512 devices in a mesh: dp: 32 (over x_hi, y, core), eigen: 16 (over x_lo, z).
Axes of the slice: x: 4 (x_hi: 2, x_lo: 2; x = x_hi * 2 + x_lo), y: 8, z: 8, core: 2. Of those that a mesh axis runs over, the one named last changes fastest.
Arguments:
- inputs: bfloat16 [128, 512, 8192], P('dp', None, 'eigen'), may hold values from -6 to 6
- output_gradients: bfloat16 [128, 512, 8192], P('dp', None, 'eigen'), may hold values from -0.5745243 to 0.5745243
- adapter_down_factor: bfloat16 [64, 8192], P(None, 'eigen'), may hold values from -0.0625 to 0.0625
- output_eigen_basis: bfloat16 [8192, 8192], P('dp', 'eigen'), may hold values from -0.0625 to 0.0625
- adapter_eigen_basis: bfloat16 [64, 64], replicated, may hold values from -0.75 to 0.75
Outputs:
- corrected: float32 [64, 8192], P(None, 'eigen')
The draws below stay inside these ranges and needn't reach their ends.
All inputs are finite; a program needn't handle non-finite values.
Results may differ from the reference program's by a relative error of at most 0.0019.
Values may be sent and summed in bfloat16 or wider, within the bound.
No kernel may reach another device: no remote copies, remote signals or barrier semaphores. Data moves between devices by JAX's collectives and lax.ppermute only.
A program may use at most 64 MiB of HBM per device.

```python
import jax
import jax.numpy as jnp
from jax import lax

MODEL_WIDTH = 8192
ADAPTER_RANK = 64
TOK_LEN = 512
EXAMPLES = 128


def draw_output_gradients(key, part):
    key_scale, key_base = jax.random.split(key, 2)
    index = jnp.arange(EXAMPLES, dtype=jnp.float32)
    ramp = 0.6 + 1.2 * index / max(EXAMPLES - 1, 1)
    factor = ramp * jax.random.uniform(key_scale, (EXAMPLES,), jnp.float32, 0.7, 1.4)
    base = jnp.clip(jax.random.normal(key_base, (EXAMPLES, TOK_LEN, MODEL_WIDTH), jnp.float32), -5.0, 5.0)
    return (base * factor[:, None, None] * TOK_LEN ** (-0.5)).astype(jnp.bfloat16)


def steps_of(rng, extent, cuts, smallest, high):
    level = 1.0
    for dim, blocks in cuts:
        heights = jax.random.uniform(jax.random.fold_in(jax.random.fold_in(rng, 6), dim), (blocks,), jnp.float32, smallest / len(cuts), high / len(cuts))
        level = level * jnp.repeat(jnp.exp(heights), extent[dim] // blocks).reshape((-1,) + (1,) * (len(extent) - 1 - dim))
    return level


def normal_values(rng, dims, spread, most, pieces=(), held_as=jnp.bfloat16):
    level = steps_of(rng, dims, pieces, -0.22, 0.18) if pieces else 1.0
    array = jax.random.normal(rng, dims, jnp.float32) * spread * level
    return jnp.minimum(jnp.maximum(array, -most), most).astype(held_as)


def setup_inputs(seed: int = 0) -> dict:
    seeds = jax.random.split(jax.random.key(seed), 6)
    return {
        "inputs": normal_values(seeds[0], (EXAMPLES, TOK_LEN, MODEL_WIDTH), 1.0, 6.0, ((0, 32), (2, 16))),
        "output_gradients": draw_output_gradients(jax.random.fold_in(seeds[5], 71), 0),
        "adapter_down_factor": normal_values(seeds[2], (ADAPTER_RANK, MODEL_WIDTH), MODEL_WIDTH ** -0.5, 0.0625, ((1, 16),)),
        "output_eigen_basis": normal_values(seeds[3], (MODEL_WIDTH, MODEL_WIDTH), MODEL_WIDTH ** -0.5, 0.0625, ((0, 32), (1, 16))),
        "adapter_eigen_basis": normal_values(seeds[4], (ADAPTER_RANK, ADAPTER_RANK), ADAPTER_RANK ** -0.5, 0.75),
    }


def reference(inputs, output_gradients, adapter_down_factor, output_eigen_basis, adapter_eigen_basis):

    def example_grad(pair):
        corrected_eigenvalues, upstream = pair
        projected_rows = jnp.dot(corrected_eigenvalues, adapter_down_factor.T, preferred_element_type=jnp.float32).astype(jnp.bfloat16)
        rotated_block = jnp.dot(projected_rows, adapter_eigen_basis, preferred_element_type=jnp.float32).astype(jnp.bfloat16)
        return jnp.dot(upstream.T, rotated_block, preferred_element_type=jnp.float32).astype(jnp.bfloat16)
    weight_gradients = lax.map(example_grad, (inputs, output_gradients))
    stacked = jnp.transpose(weight_gradients, (1, 0, 2)).reshape(MODEL_WIDTH, EXAMPLES * ADAPTER_RANK)
    coef = jnp.dot(output_eigen_basis.T, stacked, preferred_element_type=jnp.float32)
    coef = coef.reshape(MODEL_WIDTH, EXAMPLES, ADAPTER_RANK)
    squared_entries = lax.optimization_barrier(jnp.sum(coef * coef, axis=1)) / EXAMPLES
    return squared_entries.T
```

```python
import functools

import jax
import jax.numpy as jnp
from jax import lax
from jax.experimental import pallas as pl
from jax.experimental.pallas import tpu as pltpu
from jax.sharding import Mesh, PartitionSpec as P

DP = ("x_hi", "y", "core")
EIGEN = ("x_lo", "z")
SIZES = (2, 8, 2, 2, 8)
F32, BF16 = jnp.float32, jnp.bfloat16
VMEM_LIMIT = 48 * 1024 * 1024


def params(**kw):
    return pltpu.CompilerParams(vmem_limit_bytes=VMEM_LIMIT, **kw)


def project_kernel(a_ref, x_ref, o_ref):
    got = lax.dot_general(
        a_ref[...], x_ref[0], (((1,), (1,)), ((), ())), preferred_element_type=F32
    )
    for c in range(o_ref.shape[0]):
        o_ref[c] = got[:, c * 128 : (c + 1) * 128]


def project(inputs, down):
    count, tokens, width = inputs.shape
    rank = down.shape[0]
    per = tokens // 128
    return pl.pallas_call(
        project_kernel,
        grid=(count,),
        in_specs=[
            pl.BlockSpec((rank, width), lambda n: (0, 0)),
            pl.BlockSpec((1, tokens, width), lambda n: (n, 0, 0)),
        ],
        out_specs=pl.BlockSpec((per, rank, 128), lambda n: (n, 0, 0)),
        out_shape=jax.ShapeDtypeStruct((count * per, rank, 128), F32),
        compiler_params=params(),
        cost_estimate=pl.CostEstimate(
            flops=2 * count * tokens * width * rank, bytes_accessed=3 << 20, transcendentals=0
        ),
    )(down, inputs)


def rotate_kernel(p_ref, e_ref, o_ref):
    total = jnp.sum(p_ref[...], axis=0).astype(BF16)
    rot = lax.dot_general(
        e_ref[...], total, (((0,), (0,)), ((), ())), preferred_element_type=F32
    ).astype(BF16)
    for c in range(o_ref.shape[0]):
        o_ref[c] = rot


def rotate(parts, basis):
    return pl.pallas_call(
        rotate_kernel,
        out_shape=jax.ShapeDtypeStruct(parts.shape, BF16),
        compiler_params=params(),
    )(parts, basis)


def grad_kernel(ids_ref, rot_ref, dy_ref, keep_ref, send_ref):
    rot = jnp.concatenate([rot_ref[c] for c in range(rot_ref.shape[0])], axis=1)
    grad = jnp.dot(rot, dy_ref[0], preferred_element_type=F32).astype(BF16)
    half = grad.shape[1] // 2
    low, high = grad[:, :half], grad[:, half:]
    first = ids_ref[1] == 0
    keep_ref[...] = jnp.where(first, low, high)
    send_ref[...] = jnp.where(first, high, low)


def gradients(ids, rot, dy):
    count, tokens, width = dy.shape
    rank = rot.shape[1]
    per = tokens // 128
    out = jax.ShapeDtypeStruct((count * rank, width // 2), BF16)
    return pl.pallas_call(
        grad_kernel,
        grid_spec=pltpu.PrefetchScalarGridSpec(
            num_scalar_prefetch=1,
            grid=(count,),
            in_specs=[
                pl.BlockSpec((per, rank, 128), lambda n, ids: (n, 0, 0)),
                pl.BlockSpec((1, tokens, width), lambda n, ids: (n, 0, 0)),
            ],
            out_specs=[
                pl.BlockSpec((rank, width // 2), lambda n, ids: (n, 0)),
                pl.BlockSpec((rank, width // 2), lambda n, ids: (n, 0)),
            ],
        ),
        out_shape=[out, out],
        compiler_params=params(),
        cost_estimate=pl.CostEstimate(
            flops=2 * count * tokens * width * rank, bytes_accessed=3 << 20, transcendentals=0
        ),
    )(ids, rot, dy)


def coef_kernel(offsets, ids_ref, q_ref, *refs):
    pieces, (away_ref, keep_ref) = refs[:-2], refs[-2:]
    z, core = ids_ref[0], ids_ref[1]
    own = pl.ds(pl.multiple_of(core * 256, 256), 256)
    other = pl.ds(pl.multiple_of((1 - core) * 256, 256), 256)
    blocks = [lax.rem(z + off + 8, 8) for off in offsets]
    for rows, h in ((own, 0), (other, 1)):
        for cols, out in ((other, away_ref), (own, keep_ref)):
            total = None
            for piece, b in zip(pieces, blocks):
                term = jnp.dot(piece[h], q_ref[b, 0, :, cols], preferred_element_type=F32)
                total = term if total is None else total + term
            out[rows, :] = total


def coefficients(ids, which, basis, pieces, offsets):
    out = jax.ShapeDtypeStruct((512, 256), F32)
    whole = pl.BlockSpec((2, 256, 256), lambda i, ids: (0, 0, 0))
    return pl.pallas_call(
        functools.partial(coef_kernel, offsets),
        grid_spec=pltpu.PrefetchScalarGridSpec(
            num_scalar_prefetch=1,
            grid=(1,),
            in_specs=[pl.BlockSpec((8, 1, 256, 512), lambda i, ids: (0, ids[which], 0, 0))]
            + [whole] * len(pieces),
            out_specs=[pl.BlockSpec((512, 256), lambda i, ids: (0, 0))] * 2,
        ),
        out_shape=[out, out],
        compiler_params=params(),
        cost_estimate=pl.CostEstimate(flops=1 << 30, bytes_accessed=5 << 20, transcendentals=0),
    )(ids, basis, *pieces)


def square_kernel(a_ref, b_ref, c_ref, o_ref):
    coef = (a_ref[...] + b_ref[...]) + c_ref[...]
    sq = coef * coef
    rank = o_ref.shape[0]
    total = sq[:rank]
    for n in range(1, sq.shape[0] // rank):
        total = total + sq[n * rank : (n + 1) * rank]
    o_ref[...] = total


def swap(x, axis, stride=1):
    size = dict(zip(DP + EIGEN, SIZES))[axis]
    return lax.ppermute(x, axis, [(i, i ^ stride) for i in range(size)])


def shift(x, step):
    return lax.ppermute(x, "z", [(i, (i + step) % 8) for i in range(8)])


def shards(inputs, out_grads, down, out_basis, adapter_basis):
    z, core = lax.axis_index("z"), lax.axis_index("core")
    x_hi, x_lo = lax.axis_index("x_hi"), lax.axis_index("x_lo")
    mine = lax.bitwise_xor(x_hi, x_lo)
    ids = jnp.stack([z, core, mine, 1 - mine]).astype(jnp.int32)

    basis_a = lax.ppermute(out_basis, ("x_hi", "x_lo"), [(0, 0), (1, 2), (2, 1), (3, 3)])
    basis_b = lax.ppermute(out_basis, ("x_hi", "x_lo"), [(1, 0), (0, 2), (3, 1), (2, 3)])
    basis = lax.all_gather(jnp.stack([basis_a, basis_b]), "y", axis=0)

    parts = project(inputs, down)
    parts = lax.all_to_all(parts, EIGEN, 0, 0)
    rot = lax.all_to_all(rotate(parts, adapter_basis), EIGEN, 0, 0)

    keep, send = gradients(ids, rot, out_grads)
    piece = jnp.stack([keep, swap(send, "core")])
    pieces, offsets = [piece], [0]
    up = down_ = piece
    for s in range(1, 5):
        up = shift(up, 1)
        pieces.append(up)
        offsets.append(-s)
        if s < 4:
            down_ = shift(down_, -1)
            pieces.append(down_)
            offsets.append(s)

    away, keep = coefficients(ids, 3, basis, pieces, offsets)
    theirs = swap(keep + swap(away, "core"), "x_lo")
    away, keep = coefficients(ids, 2, basis, pieces, offsets)
    ours = swap(away, "core")
    total = pl.pallas_call(
        square_kernel,
        out_shape=jax.ShapeDtypeStruct((64, 256), F32),
        compiler_params=params(),
    )(keep, ours, theirs)

    total = total + swap(total, "x_hi")
    for stride in (1, 2, 4):
        total = total + swap(total, "y", stride)
    total = total * (1.0 / 128)
    other = swap(total, "core")
    first = core == 0
    return jnp.concatenate(
        [jnp.where(first, total, other), jnp.where(first, other, total)], axis=1
    )


def solution(mesh):
    fine = Mesh(mesh.devices.reshape(SIZES), DP + EIGEN)
    return jax.shard_map(
        shards,
        mesh=fine,
        in_specs=(
            P(DP, None, EIGEN),
            P(DP, None, EIGEN),
            P(None, EIGEN),
            P(DP, EIGEN),
            P(),
        ),
        out_specs=P(None, EIGEN),
        check_vma=False,
    )
```

```python
import functools

import jax
import jax.numpy as jnp
from jax import lax
from jax.experimental import pallas as pl
from jax.experimental.pallas import tpu as pltpu
from jax.sharding import Mesh, PartitionSpec as P

DP = ("x_hi", "y", "core")
EIGEN = ("x_lo", "z")
SIZES = (2, 8, 2, 2, 8)
F32, BF16 = jnp.float32, jnp.bfloat16
VMEM_LIMIT = 48 * 1024 * 1024


def params(**kw):
    return pltpu.CompilerParams(vmem_limit_bytes=VMEM_LIMIT, **kw)


WHOLE = pl.BlockSpec(memory_space=pltpu.VMEM)
SCALARS = pl.BlockSpec(memory_space=pltpu.SMEM)


def project_kernel(a_ref, x_ref, o_ref):
    per = o_ref.shape[0] // x_ref.shape[0]
    for n in range(x_ref.shape[0]):
        got = lax.dot_general(
            a_ref[...], x_ref[n], (((1,), (1,)), ((), ())), preferred_element_type=F32
        )
        for c in range(per):
            o_ref[n * per + c] = got[:, c * 128 : (c + 1) * 128].astype(o_ref.dtype)


def project(inputs, down):
    count, tokens, width = inputs.shape
    rank = down.shape[0]
    return pl.pallas_call(
        project_kernel,
        in_specs=[WHOLE, WHOLE],
        out_specs=WHOLE,
        out_shape=jax.ShapeDtypeStruct((count * tokens // 128, rank, 128), F32),
        compiler_params=params(),
        cost_estimate=pl.CostEstimate(
            flops=2 * count * tokens * width * rank, bytes_accessed=3 << 20, transcendentals=0
        ),
    )(down, inputs)


def rotate_kernel(p_ref, e_ref, o_ref):
    total = p_ref[0].astype(F32)
    for c in range(1, p_ref.shape[0]):
        total = total + p_ref[c].astype(F32)
    rot = lax.dot_general(
        e_ref[...], total.astype(BF16), (((0,), (0,)), ((), ())), preferred_element_type=F32
    ).astype(BF16)
    for c in range(o_ref.shape[0]):
        o_ref[c] = rot


def rotate(parts, basis):
    return pl.pallas_call(
        rotate_kernel,
        in_specs=[WHOLE, WHOLE],
        out_specs=WHOLE,
        out_shape=jax.ShapeDtypeStruct(parts.shape, BF16),
        compiler_params=params(),
    )(parts, basis)


def grad_kernel(ids_ref, rot_ref, dy_ref, keep_ref, send_ref):
    count, rank = dy_ref.shape[0], rot_ref.shape[1]
    per = rot_ref.shape[0] // count
    half = dy_ref.shape[2] // 2
    first = ids_ref[1] == 0
    for n in range(count):
        rot = jnp.concatenate([rot_ref[n * per + c] for c in range(per)], axis=1)
        grad = jnp.dot(rot, dy_ref[n], preferred_element_type=F32).astype(BF16)
        low, high = grad[:, :half], grad[:, half:]
        rows = slice(n * rank, (n + 1) * rank)
        keep_ref[rows, :] = jnp.where(first, low, high)
        send_ref[rows, :] = jnp.where(first, high, low)


def gradients(ids, rot, dy):
    count, tokens, width = dy.shape
    rank = rot.shape[1]
    out = jax.ShapeDtypeStruct((count * rank, width // 2), BF16)
    return pl.pallas_call(
        grad_kernel,
        in_specs=[SCALARS, WHOLE, WHOLE],
        out_specs=[WHOLE, WHOLE],
        out_shape=[out, out],
        compiler_params=params(),
        cost_estimate=pl.CostEstimate(
            flops=2 * count * tokens * width * rank, bytes_accessed=3 << 20, transcendentals=0
        ),
    )(ids, rot, dy)


def coef_kernel(offsets, which, ids_ref, q_ref, *refs):
    pieces, (away_ref, keep_ref) = refs[:-2], refs[-2:]
    z, core, mine = ids_ref[0], ids_ref[1], ids_ref[which]
    own = pl.ds(pl.multiple_of(core * 256, 256), 256)
    other = pl.ds(pl.multiple_of((1 - core) * 256, 256), 256)
    blocks = [lax.rem(z + off + 8, 8) for off in offsets]
    for rows, h in ((own, 0), (other, 1)):
        for cols, out in ((other, away_ref), (own, keep_ref)):
            total = None
            for piece, b in zip(pieces, blocks):
                term = jnp.dot(piece[h], q_ref[b, mine, :, cols], preferred_element_type=F32)
                total = term if total is None else total + term
            out[rows, :] = total


def coefficients(ids, which, basis, pieces, offsets):
    out = jax.ShapeDtypeStruct((512, 256), F32)
    return pl.pallas_call(
        functools.partial(coef_kernel, offsets, which),
        in_specs=[SCALARS] + [WHOLE] * (1 + len(pieces)),
        out_specs=[WHOLE, WHOLE],
        out_shape=[out, out],
        compiler_params=params(),
        cost_estimate=pl.CostEstimate(flops=1 << 30, bytes_accessed=5 << 20, transcendentals=0),
    )(ids, basis, *pieces)


def square_kernel(a_ref, b_ref, c_ref, o_ref):
    coef = (a_ref[...] + b_ref[...]) + c_ref[...].astype(F32)
    sq = coef * coef
    copies, rank, _ = o_ref.shape
    total = sq[:rank]
    for n in range(1, sq.shape[0] // rank):
        total = total + sq[n * rank : (n + 1) * rank]
    total = total.astype(BF16)
    for i in range(copies):
        o_ref[i] = total


def mean_kernel(p_ref, o_ref):
    total = p_ref[0].astype(F32)
    for i in range(1, p_ref.shape[0]):
        total = total + p_ref[i].astype(F32)
    o_ref[...] = total * (1.0 / 128)


def join_kernel(ids_ref, own_ref, other_ref, o_ref):
    first = ids_ref[1] == 0
    own, other = own_ref[...], other_ref[...]
    half = own.shape[1]
    o_ref[:, :half] = jnp.where(first, own, other)
    o_ref[:, half:] = jnp.where(first, other, own)


def swap(x, axis, stride=1):
    size = dict(zip(DP + EIGEN, SIZES))[axis]
    return lax.ppermute(x, axis, [(i, i ^ stride) for i in range(size)])


def shift(x, step):
    return lax.ppermute(x, "z", [(i, (i + step) % 8) for i in range(8)])


def shards(inputs, out_grads, down, out_basis, adapter_basis):
    z, core = lax.axis_index("z"), lax.axis_index("core")
    x_hi, x_lo = lax.axis_index("x_hi"), lax.axis_index("x_lo")
    mine = lax.bitwise_xor(x_hi, x_lo)
    ids = jnp.stack([z, core, mine, 1 - mine]).astype(jnp.int32)

    basis_a = lax.ppermute(out_basis, ("x_hi", "x_lo"), [(0, 0), (1, 2), (2, 1), (3, 3)])
    basis_b = lax.ppermute(out_basis, ("x_hi", "x_lo"), [(1, 0), (0, 2), (3, 1), (2, 3)])
    parts = project(inputs, down)
    parts, basis_a, basis_b = lax.optimization_barrier((parts, basis_a, basis_b))
    basis = lax.all_gather(jnp.stack([basis_a, basis_b]), "y", axis=0)

    parts = lax.all_to_all(parts, EIGEN, 0, 0)
    rot = lax.all_to_all(rotate(parts, adapter_basis), EIGEN, 0, 0)

    keep, send = gradients(ids, rot, out_grads)
    piece = jnp.stack([keep, swap(send, "core")])
    pieces, offsets = [piece], [0]
    up = down_ = piece
    for s in range(1, 5):
        if s == 4:
            up, basis = lax.optimization_barrier((up, basis))
        up = shift(up, 1)
        pieces.append(up)
        offsets.append(-s)
        if s < 4:
            down_ = shift(down_, -1)
            pieces.append(down_)
            offsets.append(s)

    away, keep = coefficients(ids, 3, basis, pieces, offsets)
    theirs = swap((keep + swap(away, "core")).astype(BF16), "x_lo")
    away, keep = coefficients(ids, 2, basis, pieces, offsets)
    ours = swap(away, "core")
    sums = pl.pallas_call(
        square_kernel,
        in_specs=[WHOLE] * 3,
        out_specs=WHOLE,
        out_shape=jax.ShapeDtypeStruct((16, 64, 256), BF16),
        compiler_params=params(),
    )(keep, ours, theirs)
    sums = lax.all_to_all(sums, ("x_hi", "y"), 0, 0)
    mean = pl.pallas_call(
        mean_kernel,
        in_specs=[WHOLE],
        out_specs=WHOLE,
        out_shape=jax.ShapeDtypeStruct((64, 256), F32),
        compiler_params=params(),
    )(sums)
    return pl.pallas_call(
        join_kernel,
        in_specs=[SCALARS, WHOLE, WHOLE],
        out_specs=WHOLE,
        out_shape=jax.ShapeDtypeStruct((64, 512), F32),
        compiler_params=params(),
    )(ids, mean, swap(mean, "core"))


def solution(mesh):
    fine = Mesh(mesh.devices.reshape(SIZES), DP + EIGEN)
    return jax.shard_map(
        shards,
        mesh=fine,
        in_specs=(
            P(DP, None, EIGEN),
            P(DP, None, EIGEN),
            P(None, EIGEN),
            P(DP, EIGEN),
            P(),
        ),
        out_specs=P(None, EIGEN),
        check_vma=False,
    )
```

```python
import functools

import jax
import jax.numpy as jnp
from jax import lax
from jax.experimental import pallas as pl
from jax.experimental.pallas import tpu as pltpu
from jax.sharding import Mesh, PartitionSpec as P

DP = ("x_hi", "y", "core")
EIGEN = ("x_lo", "z")
SIZES = (2, 8, 2, 2, 8)
F32, BF16 = jnp.float32, jnp.bfloat16
PARTIAL = BF16
VMEM_LIMIT = 16 * 1024 * 1024


def params(**kw):
    return pltpu.CompilerParams(vmem_limit_bytes=VMEM_LIMIT, **kw)


WHOLE = pl.BlockSpec(memory_space=pltpu.VMEM)
SCALARS = pl.BlockSpec(memory_space=pltpu.SMEM)


HBM = pl.BlockSpec(memory_space=pltpu.HBM)


def project_kernel(a_ref, x_ref, o_ref, a_buf, x_buf, sems):
    count = x_ref.shape[0]
    per = o_ref.shape[0] // count
    down = pltpu.make_async_copy(a_ref, a_buf, sems.at[count])
    down.start()
    copies = [pltpu.make_async_copy(x_ref.at[n], x_buf.at[n], sems.at[n]) for n in range(count)]
    for copy in copies:
        copy.start()
    down.wait()
    for n in range(count):
        copies[n].wait()
        got = lax.dot_general(
            a_buf[...], x_buf[n], (((1,), (1,)), ((), ())), preferred_element_type=F32
        )
        for c in range(per):
            o_ref[n * per + c] = got[:, c * 128 : (c + 1) * 128].astype(o_ref.dtype)


def project(inputs, down):
    count, tokens, width = inputs.shape
    rank = down.shape[0]
    return pl.pallas_call(
        project_kernel,
        in_specs=[HBM, HBM],
        out_specs=WHOLE,
        out_shape=jax.ShapeDtypeStruct((count * tokens // 128, rank, 128), PARTIAL),
        scratch_shapes=[
            pltpu.VMEM(down.shape, BF16),
            pltpu.VMEM(inputs.shape, BF16),
            pltpu.SemaphoreType.DMA((count + 1,)),
        ],
        compiler_params=pltpu.CompilerParams(vmem_limit_bytes=60 * 1024 * 1024),
        cost_estimate=pl.CostEstimate(
            flops=2 * count * tokens * width * rank, bytes_accessed=3 << 20, transcendentals=0
        ),
    )(down, inputs)


def rotate_kernel(p_ref, e_ref, o_ref):
    total = p_ref[0].astype(F32)
    for c in range(1, p_ref.shape[0]):
        total = total + p_ref[c].astype(F32)
    rot = lax.dot_general(
        e_ref[...], total.astype(BF16), (((0,), (0,)), ((), ())), preferred_element_type=F32
    ).astype(BF16)
    for c in range(o_ref.shape[0]):
        o_ref[c] = rot


def rotate(parts, basis):
    return pl.pallas_call(
        rotate_kernel,
        in_specs=[WHOLE, WHOLE],
        out_specs=WHOLE,
        out_shape=jax.ShapeDtypeStruct(parts.shape, BF16),
        compiler_params=params(),
    )(parts, basis)


def grad_kernel(ids_ref, rot_ref, dy_ref, keep_ref, send_ref):
    count, rank = dy_ref.shape[0], rot_ref.shape[1]
    per = rot_ref.shape[0] // count
    half = dy_ref.shape[2] // 2
    first = ids_ref[1] == 0
    for n in range(count):
        rot = jnp.concatenate([rot_ref[n * per + c] for c in range(per)], axis=1)
        grad = jnp.dot(rot, dy_ref[n], preferred_element_type=F32).astype(BF16)
        low, high = grad[:, :half], grad[:, half:]
        rows = slice(n * rank, (n + 1) * rank)
        keep_ref[rows, :] = jnp.where(first, low, high)
        send_ref[rows, :] = jnp.where(first, high, low)


def gradients(ids, rot, dy):
    count, tokens, width = dy.shape
    rank = rot.shape[1]
    out = jax.ShapeDtypeStruct((count * rank, width // 2), BF16)
    return pl.pallas_call(
        grad_kernel,
        in_specs=[SCALARS, WHOLE, WHOLE],
        out_specs=[WHOLE, WHOLE],
        out_shape=[out, out],
        compiler_params=params(),
        cost_estimate=pl.CostEstimate(
            flops=2 * count * tokens * width * rank, bytes_accessed=3 << 20, transcendentals=0
        ),
    )(ids, rot, dy)


def coef_parts(ids_ref, q_ref, pieces, offsets, dests):
    z, x_hi, x_lo = ids_ref[0], ids_ref[1], ids_ref[2]
    blocks = [lax.rem(z + off + 8, 8) for off in offsets]
    for i, (other_hi, other_lo) in enumerate(dests):
        j = 1 - x_lo if other_lo else x_lo
        half = 1 - x_hi if other_hi else x_hi
        cols = pl.ds(pl.multiple_of(half * 256, 256), 256)
        for h in range(2):
            rows = pl.ds(pl.multiple_of((1 - x_lo if h else x_lo) * 256, 256), 256)
            total = None
            for piece, b in zip(pieces, blocks):
                term = jnp.dot(piece[h], q_ref[b, j, :, cols], preferred_element_type=F32)
                total = term if total is None else total + term
            yield i, rows, total


DESTS = ((1, 0), (0, 1), (1, 1), (0, 0))
COEF = (512, 256)


def early_kernel(offsets, ids_ref, q_ref, *refs):
    pieces, out = refs[:-1], refs[-1]
    for i, rows, total in coef_parts(ids_ref, q_ref, pieces, offsets, DESTS):
        out[i, rows, :] = total


def late_kernel(offset, first, count, ids_ref, q_ref, piece_ref, sum_ref, *outs):
    dests = DESTS[first : first + count]
    for i, rows, total in coef_parts(ids_ref, q_ref, [piece_ref], [offset], dests):
        outs[i][rows, :] = (sum_ref[first + i, rows, :] + total).astype(outs[i].dtype)


def early(ids, basis, pieces, offsets):
    return pl.pallas_call(
        functools.partial(early_kernel, offsets),
        in_specs=[SCALARS] + [WHOLE] * (1 + len(pieces)),
        out_specs=WHOLE,
        out_shape=jax.ShapeDtypeStruct((4,) + COEF, F32),
        compiler_params=params(),
        cost_estimate=pl.CostEstimate(flops=2 << 30, bytes_accessed=8 << 20, transcendentals=0),
    )(ids, basis, *pieces)


def late(ids, basis, piece, offset, sums, first, count, dtype):
    return pl.pallas_call(
        functools.partial(late_kernel, offset, first, count),
        in_specs=[SCALARS] + [WHOLE] * 3,
        out_specs=[WHOLE] * count,
        out_shape=[jax.ShapeDtypeStruct(COEF, dtype)] * count,
        compiler_params=params(),
        cost_estimate=pl.CostEstimate(flops=1 << 28, bytes_accessed=2 << 20, transcendentals=0),
    )(ids, basis, piece, sums)


def square_kernel(a_ref, b_ref, c_ref, d_ref, o_ref):
    coef = (a_ref[...] + b_ref[...].astype(F32)) + (c_ref[...].astype(F32) + d_ref[...].astype(F32))
    sq = coef * coef
    rank = o_ref.shape[1]
    total = sq[:rank]
    for n in range(1, sq.shape[0] // rank):
        total = total + sq[n * rank : (n + 1) * rank]
    total = total.astype(BF16)
    for i in range(o_ref.shape[0]):
        o_ref[i] = total


def mean_kernel(p_ref, o_ref):
    total = p_ref[0].astype(F32)
    for i in range(1, p_ref.shape[0]):
        total = total + p_ref[i].astype(F32)
    o_ref[...] = total * (1.0 / 128)


def join_kernel(ids_ref, own_ref, core_ref, hi_ref, both_ref, o_ref):
    first = ids_ref[1] == 0
    own, other = own_ref[...] + core_ref[...], hi_ref[...] + both_ref[...]
    half = own.shape[1]
    o_ref[:, :half] = jnp.where(first, own, other)
    o_ref[:, half:] = jnp.where(first, other, own)


def swap(x, axis, stride=1):
    size = dict(zip(DP + EIGEN, SIZES))[axis]
    return lax.ppermute(x, axis, [(i, i ^ stride) for i in range(size)])


def shift(x, step):
    return lax.ppermute(x, "z", [(i, (i + step) % 8) for i in range(8)])


TURN = [(0, 0), (1, 2), (2, 1), (3, 3)]
CROSS = [(2, 0), (0, 1), (3, 2), (1, 3)]


def shards(inputs, out_grads, down, out_basis, adapter_basis):
    z = lax.axis_index("z")
    x_hi, x_lo = lax.axis_index("x_hi"), lax.axis_index("x_lo")
    ids = jnp.stack([z, x_hi, x_lo]).astype(jnp.int32)

    turned = lax.ppermute(out_basis, ("core", "x_lo"), TURN)
    parts = project(inputs, down)
    parts = lax.all_to_all(parts, EIGEN, 0, 0)
    parts, turned = lax.optimization_barrier((parts, turned))
    basis = lax.all_gather(turned, ("y", "core"), axis=0).reshape(8, 2, *out_basis.shape)
    rot = lax.all_to_all(rotate(parts, adapter_basis), EIGEN, 0, 0)

    keep, send = gradients(ids, rot, out_grads)
    send = lax.ppermute(send, ("x_hi", "x_lo"), CROSS)
    keep = lax.ppermute(keep, ("x_hi", "x_lo"), TURN)
    piece = jnp.stack([keep, send])
    pieces, offsets = [piece], [0]
    up = down_ = piece
    for s in range(1, 4):
        up, down_ = shift(up, 1), shift(down_, -1)
        pieces += [up, down_]
        offsets += [-s, s]
    last = shift(up, 1)

    sums = early(ids, basis, pieces, offsets)
    (far,) = late(ids, basis, last, 4, sums, 0, 1, BF16)
    beside, across = late(ids, basis, last, 4, sums, 1, 2, BF16)
    (keep,) = late(ids, basis, last, 4, sums, 3, 1, F32)
    far = swap(far, "x_hi")
    beside = swap(beside, "x_lo")
    across = lax.ppermute(across, ("x_hi", "x_lo"), [(0, 3), (1, 2), (2, 1), (3, 0)])
    sums = pl.pallas_call(
        square_kernel,
        in_specs=[WHOLE] * 4,
        out_specs=WHOLE,
        out_shape=jax.ShapeDtypeStruct((8, 64, 256), BF16),
        compiler_params=params(),
    )(keep, far, beside, across)
    sums = lax.all_to_all(sums, "y", 0, 0)
    mean = pl.pallas_call(
        mean_kernel,
        in_specs=[WHOLE],
        out_specs=WHOLE,
        out_shape=jax.ShapeDtypeStruct((64, 256), F32),
        compiler_params=params(),
    )(sums)
    both = lax.ppermute(mean, ("x_hi", "core"), [(0, 3), (1, 2), (2, 1), (3, 0)])
    return pl.pallas_call(
        join_kernel,
        in_specs=[SCALARS] + [WHOLE] * 4,
        out_specs=WHOLE,
        out_shape=jax.ShapeDtypeStruct((64, 512), F32),
        compiler_params=params(),
    )(ids, mean, swap(mean, "core"), swap(mean, "x_hi"), both)


def solution(mesh):
    fine = Mesh(mesh.devices.reshape(SIZES), DP + EIGEN)
    return jax.shard_map(
        shards,
        mesh=fine,
        in_specs=(
            P(DP, None, EIGEN),
            P(DP, None, EIGEN),
            P(None, EIGEN),
            P(DP, EIGEN),
            P(),
        ),
        out_specs=P(None, EIGEN),
        check_vma=False,
    )
```

```python
import functools

import jax
import jax.numpy as jnp
from jax import lax
from jax.experimental import pallas as pl
from jax.experimental.pallas import tpu as pltpu
from jax.sharding import Mesh, PartitionSpec as P

DP = ("x_hi", "y", "core")
EIGEN = ("x_lo", "z")
SIZES = (2, 8, 2, 2, 8)
F32, BF16 = jnp.float32, jnp.bfloat16
PARTIAL = BF16
VMEM_LIMIT = 16 * 1024 * 1024


def params(**kw):
    return pltpu.CompilerParams(vmem_limit_bytes=VMEM_LIMIT, **kw)


WHOLE = pl.BlockSpec(memory_space=pltpu.VMEM)
SCALARS = pl.BlockSpec(memory_space=pltpu.SMEM)


HBM = pl.BlockSpec(memory_space=pltpu.HBM)


def project_kernel(a_ref, x_ref, o_ref, a_buf, x_buf, sems):
    count = x_ref.shape[0]
    per = o_ref.shape[0] // count
    down = pltpu.make_async_copy(a_ref, a_buf, sems.at[count])
    down.start()
    copies = [pltpu.make_async_copy(x_ref.at[n], x_buf.at[n], sems.at[n]) for n in range(count)]
    for copy in copies:
        copy.start()
    down.wait()
    for n in range(count):
        copies[n].wait()
        got = lax.dot_general(
            a_buf[...], x_buf[n], (((1,), (1,)), ((), ())), preferred_element_type=F32
        )
        for c in range(per):
            o_ref[n * per + c] = got[:, c * 128 : (c + 1) * 128].astype(o_ref.dtype)


def project(inputs, down):
    count, tokens, width = inputs.shape
    rank = down.shape[0]
    return pl.pallas_call(
        project_kernel,
        in_specs=[HBM, HBM],
        out_specs=WHOLE,
        out_shape=jax.ShapeDtypeStruct((count * tokens // 128, rank, 128), PARTIAL),
        scratch_shapes=[
            pltpu.VMEM(down.shape, BF16),
            pltpu.VMEM(inputs.shape, BF16),
            pltpu.SemaphoreType.DMA((count + 1,)),
        ],
        compiler_params=pltpu.CompilerParams(vmem_limit_bytes=60 * 1024 * 1024),
        cost_estimate=pl.CostEstimate(
            flops=2 * count * tokens * width * rank, bytes_accessed=3 << 20, transcendentals=0
        ),
    )(down, inputs)


def rotate_kernel(p_ref, e_ref, o_ref):
    total = p_ref[0].astype(F32)
    for c in range(1, p_ref.shape[0]):
        total = total + p_ref[c].astype(F32)
    rot = lax.dot_general(
        e_ref[...], total.astype(BF16), (((0,), (0,)), ((), ())), preferred_element_type=F32
    ).astype(BF16)
    for c in range(o_ref.shape[0]):
        o_ref[c] = rot


def rotate(parts, basis):
    return pl.pallas_call(
        rotate_kernel,
        in_specs=[WHOLE, WHOLE],
        out_specs=WHOLE,
        out_shape=jax.ShapeDtypeStruct(parts.shape, BF16),
        compiler_params=params(),
    )(parts, basis)


def grad_kernel(ids_ref, rot_ref, dy_ref, keep_ref, send_ref):
    count, rank = dy_ref.shape[0], rot_ref.shape[1]
    per = rot_ref.shape[0] // count
    half = dy_ref.shape[2] // 2
    first = ids_ref[1] == 0
    for n in range(count):
        rot = jnp.concatenate([rot_ref[n * per + c] for c in range(per)], axis=1)
        grad = jnp.dot(rot, dy_ref[n], preferred_element_type=F32).astype(BF16)
        low, high = grad[:, :half], grad[:, half:]
        rows = slice(n * rank, (n + 1) * rank)
        keep_ref[rows, :] = jnp.where(first, low, high)
        send_ref[rows, :] = jnp.where(first, high, low)


def gradients(ids, rot, dy):
    count, tokens, width = dy.shape
    rank = rot.shape[1]
    out = jax.ShapeDtypeStruct((count * rank, width // 2), BF16)
    return pl.pallas_call(
        grad_kernel,
        in_specs=[SCALARS, WHOLE, WHOLE],
        out_specs=[WHOLE, WHOLE],
        out_shape=[out, out],
        compiler_params=params(),
        cost_estimate=pl.CostEstimate(
            flops=2 * count * tokens * width * rank, bytes_accessed=3 << 20, transcendentals=0
        ),
    )(ids, rot, dy)


def coef_parts(ids_ref, q_ref, pieces, offsets, dests):
    z, x_hi, x_lo = ids_ref[0], ids_ref[1], ids_ref[2]
    blocks = [lax.rem(z + off + 8, 8) for off in offsets]
    for i, (other_hi, other_lo) in enumerate(dests):
        j = 1 - x_lo if other_lo else x_lo
        half = 1 - x_hi if other_hi else x_hi
        cols = pl.ds(pl.multiple_of(half * 256, 256), 256)
        for h in range(2):
            rows = pl.ds(pl.multiple_of((1 - x_lo if h else x_lo) * 256, 256), 256)
            total = None
            for piece, b in zip(pieces, blocks):
                term = jnp.dot(piece[h], q_ref[b, j, :, cols], preferred_element_type=F32)
                total = term if total is None else total + term
            yield i, rows, total


DESTS = ((1, 0), (0, 1), (1, 1), (0, 0))
COEF = (512, 256)


def early_kernel(offsets, ids_ref, q_ref, *refs):
    pieces, out = refs[:-1], refs[-1]
    for i, rows, total in coef_parts(ids_ref, q_ref, pieces, offsets, DESTS):
        out[i, rows, :] = total


def late_kernel(offset, ids_ref, q_ref, piece_ref, sum_ref, away_ref, keep_ref):
    for i, rows, total in coef_parts(ids_ref, q_ref, [piece_ref], [offset], DESTS):
        total = sum_ref[i, rows, :] + total
        if i == 3:
            keep_ref[rows, :] = total
        hi, lo = DESTS[i]
        slot = (1 - ids_ref[1] if hi else ids_ref[1]) * 2 + (1 - ids_ref[2] if lo else ids_ref[2])
        away_ref[slot, rows, :] = total.astype(BF16)


def early(ids, basis, pieces, offsets):
    return pl.pallas_call(
        functools.partial(early_kernel, offsets),
        in_specs=[SCALARS] + [WHOLE] * (1 + len(pieces)),
        out_specs=WHOLE,
        out_shape=jax.ShapeDtypeStruct((4,) + COEF, F32),
        compiler_params=params(),
        cost_estimate=pl.CostEstimate(flops=2 << 30, bytes_accessed=8 << 20, transcendentals=0),
    )(ids, basis, *pieces)


def late(ids, basis, piece, offset, sums):
    return pl.pallas_call(
        functools.partial(late_kernel, offset),
        in_specs=[SCALARS] + [WHOLE] * 3,
        out_specs=[WHOLE] * 2,
        out_shape=[
            jax.ShapeDtypeStruct((4,) + COEF, BF16),
            jax.ShapeDtypeStruct(COEF, F32),
        ],
        compiler_params=params(),
        cost_estimate=pl.CostEstimate(flops=1 << 28, bytes_accessed=2 << 20, transcendentals=0),
    )(ids, basis, piece, sums)


def square_kernel(ids_ref, keep_ref, p_ref, o_ref):
    x_hi, x_lo = ids_ref[1], ids_ref[2]
    far, beside = 2 * (1 - x_hi) + x_lo, 2 * x_hi + 1 - x_lo
    across = 2 * (1 - x_hi) + 1 - x_lo
    coef = keep_ref[...]
    for slot in (far, beside, across):
        coef = coef + p_ref[slot].astype(F32)
    sq = coef * coef
    rank = o_ref.shape[1]
    total = sq[:rank]
    for n in range(1, sq.shape[0] // rank):
        total = total + sq[n * rank : (n + 1) * rank]
    total = total.astype(BF16)
    for i in range(o_ref.shape[0]):
        o_ref[i] = total


def mean_kernel(p_ref, o_ref):
    total = p_ref[0].astype(F32)
    for i in range(1, p_ref.shape[0]):
        total = total + p_ref[i].astype(F32)
    total = total * (1.0 / 128)
    for i in range(o_ref.shape[0]):
        o_ref[i] = total


def join_kernel(p_ref, o_ref):
    half = p_ref.shape[2]
    for h in range(2):
        o_ref[:, h * half : (h + 1) * half] = p_ref[2 * h] + p_ref[2 * h + 1]


def swap(x, axis, stride=1):
    size = dict(zip(DP + EIGEN, SIZES))[axis]
    return lax.ppermute(x, axis, [(i, i ^ stride) for i in range(size)])


def shift(x, step):
    return lax.ppermute(x, "z", [(i, (i + step) % 8) for i in range(8)])


TURN = [(0, 0), (1, 2), (2, 1), (3, 3)]
CROSS = [(2, 0), (0, 1), (3, 2), (1, 3)]


def shards(inputs, out_grads, down, out_basis, adapter_basis):
    z = lax.axis_index("z")
    x_hi, x_lo = lax.axis_index("x_hi"), lax.axis_index("x_lo")
    ids = jnp.stack([z, x_hi, x_lo]).astype(jnp.int32)

    turned = lax.ppermute(out_basis, ("core", "x_lo"), TURN)
    parts = project(inputs, down)
    parts = lax.all_to_all(parts, EIGEN, 0, 0)
    parts, turned = lax.optimization_barrier((parts, turned))
    basis = lax.all_gather(turned, ("y", "core"), axis=0).reshape(8, 2, *out_basis.shape)
    rot = lax.all_to_all(rotate(parts, adapter_basis), EIGEN, 0, 0)

    keep, send = gradients(ids, rot, out_grads)
    send = lax.ppermute(send, ("x_hi", "x_lo"), CROSS)
    keep = lax.ppermute(keep, ("x_hi", "x_lo"), TURN)
    piece = jnp.stack([keep, send])
    pieces, offsets = [piece], [0]
    up = down_ = piece
    for s in range(1, 4):
        up, down_ = shift(up, 1), shift(down_, -1)
        pieces += [up, down_]
        offsets += [-s, s]
    last = shift(up, 1)

    sums = early(ids, basis, pieces, offsets)
    away, keep = late(ids, basis, last, 4, sums)
    away = lax.all_to_all(away, ("x_hi", "x_lo"), 0, 0)
    sums = pl.pallas_call(
        square_kernel,
        in_specs=[SCALARS] + [WHOLE] * 2,
        out_specs=WHOLE,
        out_shape=jax.ShapeDtypeStruct((8, 64, 256), BF16),
        compiler_params=params(),
    )(ids, keep, away)
    sums = lax.all_to_all(sums, "y", 0, 0)
    mean = pl.pallas_call(
        mean_kernel,
        in_specs=[WHOLE],
        out_specs=WHOLE,
        out_shape=jax.ShapeDtypeStruct((4, 64, 256), F32),
        compiler_params=params(),
    )(sums)
    mean = lax.all_to_all(mean, ("x_hi", "core"), 0, 0)
    return pl.pallas_call(
        join_kernel,
        in_specs=[WHOLE],
        out_specs=WHOLE,
        out_shape=jax.ShapeDtypeStruct((64, 512), F32),
        compiler_params=params(),
    )(mean)


def solution(mesh):
    fine = Mesh(mesh.devices.reshape(SIZES), DP + EIGEN)
    return jax.shard_map(
        shards,
        mesh=fine,
        in_specs=(
            P(DP, None, EIGEN),
            P(DP, None, EIGEN),
            P(None, EIGEN),
            P(DP, EIGEN),
            P(),
        ),
        out_specs=P(None, EIGEN),
        check_vma=False,
    )
```

```python
import functools

import jax
import jax.numpy as jnp
from jax import lax
from jax.experimental import pallas as pl
from jax.experimental.pallas import tpu as pltpu
from jax.sharding import Mesh, PartitionSpec as P

DP = ("x_hi", "y", "core")
EIGEN = ("x_lo", "z")
SIZES = (2, 8, 2, 2, 8)
F32, BF16 = jnp.float32, jnp.bfloat16
PARTIAL = BF16
VMEM_LIMIT = 16 * 1024 * 1024


def params(**kw):
    return pltpu.CompilerParams(vmem_limit_bytes=VMEM_LIMIT, **kw)


WHOLE = pl.BlockSpec(memory_space=pltpu.VMEM)
SCALARS = pl.BlockSpec(memory_space=pltpu.SMEM)


HBM = pl.BlockSpec(memory_space=pltpu.HBM)


def project_kernel(a_ref, x_ref, o_ref, a_buf, x_buf, sems):
    count = x_ref.shape[0]
    per = o_ref.shape[0] // count
    down = pltpu.make_async_copy(a_ref, a_buf, sems.at[count])
    down.start()
    copies = [pltpu.make_async_copy(x_ref.at[n], x_buf.at[n], sems.at[n]) for n in range(count)]
    for copy in copies:
        copy.start()
    down.wait()
    for n in range(count):
        copies[n].wait()
        got = lax.dot_general(
            a_buf[...], x_buf[n], (((1,), (1,)), ((), ())), preferred_element_type=F32
        )
        for c in range(per):
            o_ref[n * per + c] = got[:, c * 128 : (c + 1) * 128].astype(o_ref.dtype)


def project(inputs, down):
    count, tokens, width = inputs.shape
    rank = down.shape[0]
    return pl.pallas_call(
        project_kernel,
        in_specs=[HBM, HBM],
        out_specs=WHOLE,
        out_shape=jax.ShapeDtypeStruct((count * tokens // 128, rank, 128), PARTIAL),
        scratch_shapes=[
            pltpu.VMEM(down.shape, BF16),
            pltpu.VMEM(inputs.shape, BF16),
            pltpu.SemaphoreType.DMA((count + 1,)),
        ],
        compiler_params=pltpu.CompilerParams(vmem_limit_bytes=60 * 1024 * 1024),
        cost_estimate=pl.CostEstimate(
            flops=2 * count * tokens * width * rank, bytes_accessed=3 << 20, transcendentals=0
        ),
    )(down, inputs)


def rotate_kernel(p_ref, e_ref, o_ref):
    total = p_ref[0].astype(F32)
    for c in range(1, p_ref.shape[0]):
        total = total + p_ref[c].astype(F32)
    rot = lax.dot_general(
        e_ref[...], total.astype(BF16), (((0,), (0,)), ((), ())), preferred_element_type=F32
    ).astype(BF16)
    for c in range(o_ref.shape[0]):
        o_ref[c] = rot


def rotate(parts, basis):
    return pl.pallas_call(
        rotate_kernel,
        in_specs=[WHOLE, WHOLE],
        out_specs=WHOLE,
        out_shape=jax.ShapeDtypeStruct(parts.shape, BF16),
        compiler_params=params(),
    )(parts, basis)


def grad_kernel(rot_ref, dy_ref, o_ref):
    count, rank = dy_ref.shape[0], rot_ref.shape[1]
    per = rot_ref.shape[0] // count
    half = dy_ref.shape[2] // 2
    for n in range(count):
        rot = jnp.concatenate([rot_ref[n * per + c] for c in range(per)], axis=1)
        grad = jnp.dot(rot, dy_ref[n], preferred_element_type=F32).astype(BF16)
        rows = slice(n * rank, (n + 1) * rank)
        for h in range(2):
            o_ref[h, rows, :] = grad[:, h * half : (h + 1) * half]


def gradients(rot, dy):
    count, tokens, width = dy.shape
    rank = rot.shape[1]
    return pl.pallas_call(
        grad_kernel,
        in_specs=[WHOLE, WHOLE],
        out_specs=WHOLE,
        out_shape=jax.ShapeDtypeStruct((2, count * rank, width // 2), BF16),
        compiler_params=params(),
        cost_estimate=pl.CostEstimate(
            flops=2 * count * tokens * width * rank, bytes_accessed=3 << 20, transcendentals=0
        ),
    )(rot, dy)


def coef_parts(ids_ref, q_ref, pieces, offsets, dests):
    z, x_hi, x_lo = ids_ref[0], ids_ref[1], ids_ref[2]
    blocks = [lax.rem(z + off + 8, 8) for off in offsets]
    for i, (other_hi, other_lo) in enumerate(dests):
        j = 1 - x_lo if other_lo else x_lo
        half = 1 - x_hi if other_hi else x_hi
        cols = pl.ds(pl.multiple_of(half * 256, 256), 256)
        for h in range(2):
            rows = slice(256 * h, 256 * h + 256)
            total = None
            for piece, b in zip(pieces, blocks):
                term = jnp.dot(piece[h], q_ref[b, j, :, cols], preferred_element_type=F32)
                total = term if total is None else total + term
            yield i, rows, total


DESTS = ((1, 0), (0, 1), (1, 1), (0, 0))
COEF = (512, 256)


def early_kernel(offsets, ids_ref, q_ref, *refs):
    pieces, out = refs[:-1], refs[-1]
    for i, rows, total in coef_parts(ids_ref, q_ref, pieces, offsets, DESTS):
        out[i, rows, :] = total


def late_kernel(offset, ids_ref, q_ref, piece_ref, sum_ref, away_ref, keep_ref):
    for i, rows, total in coef_parts(ids_ref, q_ref, [piece_ref], [offset], DESTS):
        total = sum_ref[i, rows, :] + total
        if i == 3:
            keep_ref[rows, :] = total
        hi, lo = DESTS[i]
        slot = (1 - ids_ref[1] if hi else ids_ref[1]) * 2 + (1 - ids_ref[2] if lo else ids_ref[2])
        away_ref[slot, rows, :] = total.astype(BF16)


def early(ids, basis, pieces, offsets):
    return pl.pallas_call(
        functools.partial(early_kernel, offsets),
        in_specs=[SCALARS] + [WHOLE] * (1 + len(pieces)),
        out_specs=WHOLE,
        out_shape=jax.ShapeDtypeStruct((4,) + COEF, F32),
        compiler_params=params(),
        cost_estimate=pl.CostEstimate(flops=2 << 30, bytes_accessed=8 << 20, transcendentals=0),
    )(ids, basis, *pieces)


def late(ids, basis, piece, offset, sums):
    return pl.pallas_call(
        functools.partial(late_kernel, offset),
        in_specs=[SCALARS] + [WHOLE] * 3,
        out_specs=[WHOLE] * 2,
        out_shape=[
            jax.ShapeDtypeStruct((4,) + COEF, BF16),
            jax.ShapeDtypeStruct(COEF, F32),
        ],
        compiler_params=params(),
        cost_estimate=pl.CostEstimate(flops=1 << 28, bytes_accessed=2 << 20, transcendentals=0),
    )(ids, basis, piece, sums)


def square_kernel(ids_ref, keep_ref, p_ref, o_ref):
    x_hi, x_lo = ids_ref[1], ids_ref[2]
    far, beside = 2 * (1 - x_hi) + x_lo, 2 * x_hi + 1 - x_lo
    across = 2 * (1 - x_hi) + 1 - x_lo
    coef = keep_ref[...]
    for slot in (far, beside, across):
        coef = coef + p_ref[slot].astype(F32)
    sq = coef * coef
    rank = o_ref.shape[1]
    total = sq[:rank]
    for n in range(1, sq.shape[0] // rank):
        total = total + sq[n * rank : (n + 1) * rank]
    total = total.astype(BF16)
    for i in range(o_ref.shape[0]):
        o_ref[i] = total


def mean_kernel(p_ref, o_ref):
    total = p_ref[0].astype(F32)
    for i in range(1, p_ref.shape[0]):
        total = total + p_ref[i].astype(F32)
    o_ref[...] = total * (1.0 / 128)


def join_kernel(p_ref, o_ref):
    half = p_ref.shape[2]
    for h in range(2):
        o_ref[:, h * half : (h + 1) * half] = p_ref[2 * h] + p_ref[2 * h + 1]


def swap(x, axis, stride=1):
    size = dict(zip(DP + EIGEN, SIZES))[axis]
    return lax.ppermute(x, axis, [(i, i ^ stride) for i in range(size)])


def shift(x, step):
    return lax.ppermute(x, "z", [(i, (i + step) % 8) for i in range(8)])


TURN = [(4 * h + 2 * c + l, 4 * c + 2 * l + h) for h in range(2) for c in range(2) for l in range(2)]


def shards(inputs, out_grads, down, out_basis, adapter_basis):
    z = lax.axis_index("z")
    x_hi, x_lo = lax.axis_index("x_hi"), lax.axis_index("x_lo")
    ids = jnp.stack([z, x_hi, x_lo]).astype(jnp.int32)

    turned = lax.ppermute(out_basis, ("x_hi", "core", "x_lo"), TURN)
    parts = project(inputs, down)
    parts = lax.all_to_all(parts, EIGEN, 0, 0)
    parts = rotate(parts, adapter_basis)
    parts, turned = lax.optimization_barrier((parts, turned))
    basis = lax.all_gather(turned, ("y", "core"), axis=0).reshape(8, 2, *out_basis.shape)
    rot = lax.all_to_all(parts, EIGEN, 0, 0)

    piece = lax.all_to_all(gradients(rot, out_grads), "x_hi", 0, 0)
    pieces, offsets = [piece], [0]
    up = down_ = piece
    for s in range(1, 4):
        up, down_ = shift(up, 1), shift(down_, -1)
        pieces += [up, down_]
        offsets += [-s, s]
    last = shift(up, 1)

    sums = early(ids, basis, pieces, offsets)
    away, keep = late(ids, basis, last, 4, sums)
    away = lax.all_to_all(away, ("x_hi", "x_lo"), 0, 0)
    sums = pl.pallas_call(
        square_kernel,
        in_specs=[SCALARS] + [WHOLE] * 2,
        out_specs=WHOLE,
        out_shape=jax.ShapeDtypeStruct((8, 64, 256), BF16),
        compiler_params=params(),
    )(ids, keep, away)
    sums = lax.all_to_all(sums, "y", 0, 0)
    mean = pl.pallas_call(
        mean_kernel,
        in_specs=[WHOLE],
        out_specs=WHOLE,
        out_shape=jax.ShapeDtypeStruct((64, 256), F32),
        compiler_params=params(),
    )(sums)
    mean = lax.all_gather(mean, ("x_hi", "core"), axis=0)
    return pl.pallas_call(
        join_kernel,
        in_specs=[WHOLE],
        out_specs=WHOLE,
        out_shape=jax.ShapeDtypeStruct((64, 512), F32),
        compiler_params=params(),
    )(mean)


def solution(mesh):
    fine = Mesh(mesh.devices.reshape(SIZES), DP + EIGEN)
    return jax.shard_map(
        shards,
        mesh=fine,
        in_specs=(
            P(DP, None, EIGEN),
            P(DP, None, EIGEN),
            P(None, EIGEN),
            P(DP, EIGEN),
            P(),
        ),
        out_specs=P(None, EIGEN),
        check_vma=False,
    )
```

```python
import functools

import jax
import jax.numpy as jnp
from jax import lax
from jax.experimental import pallas as pl
from jax.experimental.pallas import tpu as pltpu
from jax.sharding import Mesh, PartitionSpec as P

DP = ("x_hi", "y", "core")
EIGEN = ("x_lo", "z")
SIZES = (2, 8, 2, 2, 8)
F32, BF16 = jnp.float32, jnp.bfloat16
PARTIAL = BF16
VMEM_LIMIT = 16 * 1024 * 1024


def params(**kw):
    return pltpu.CompilerParams(vmem_limit_bytes=VMEM_LIMIT, **kw)


WHOLE = pl.BlockSpec(memory_space=pltpu.VMEM)
SCALARS = pl.BlockSpec(memory_space=pltpu.SMEM)


HBM = pl.BlockSpec(memory_space=pltpu.HBM)


def project_kernel(a_ref, x_ref, o_ref, a_buf, x_buf, sems):
    count = x_ref.shape[0]
    per = o_ref.shape[0] // count
    down = pltpu.make_async_copy(a_ref, a_buf, sems.at[count])
    down.start()
    copies = [pltpu.make_async_copy(x_ref.at[n], x_buf.at[n], sems.at[n]) for n in range(count)]
    for copy in copies:
        copy.start()
    down.wait()
    for n in range(count):
        copies[n].wait()
        got = lax.dot_general(
            a_buf[...], x_buf[n], (((1,), (1,)), ((), ())), preferred_element_type=F32
        )
        for c in range(per):
            o_ref[n * per + c] = got[:, c * 128 : (c + 1) * 128].astype(o_ref.dtype)


def project(inputs, down):
    count, tokens, width = inputs.shape
    rank = down.shape[0]
    return pl.pallas_call(
        project_kernel,
        in_specs=[HBM, HBM],
        out_specs=WHOLE,
        out_shape=jax.ShapeDtypeStruct((count * tokens // 128, rank, 128), PARTIAL),
        scratch_shapes=[
            pltpu.VMEM(down.shape, BF16),
            pltpu.VMEM(inputs.shape, BF16),
            pltpu.SemaphoreType.DMA((count + 1,)),
        ],
        compiler_params=pltpu.CompilerParams(vmem_limit_bytes=60 * 1024 * 1024),
        cost_estimate=pl.CostEstimate(
            flops=2 * count * tokens * width * rank, bytes_accessed=3 << 20, transcendentals=0
        ),
    )(down, inputs)


def rotate_kernel(p_ref, e_ref, o_ref):
    total = p_ref[0].astype(F32)
    for c in range(1, p_ref.shape[0]):
        total = total + p_ref[c].astype(F32)
    rot = lax.dot_general(
        e_ref[...], total.astype(BF16), (((0,), (0,)), ((), ())), preferred_element_type=F32
    ).astype(BF16)
    for c in range(o_ref.shape[0]):
        o_ref[c] = rot


def rotate(parts, basis):
    return pl.pallas_call(
        rotate_kernel,
        in_specs=[WHOLE, WHOLE],
        out_specs=WHOLE,
        out_shape=jax.ShapeDtypeStruct(parts.shape, BF16),
        compiler_params=params(),
    )(parts, basis)


def grad_kernel(rot_ref, dy_ref, o_ref):
    count, rank = dy_ref.shape[0], rot_ref.shape[1]
    per = rot_ref.shape[0] // count
    half = dy_ref.shape[2] // 2
    for n in range(count):
        rot = jnp.concatenate([rot_ref[n * per + c] for c in range(per)], axis=1)
        grad = jnp.dot(rot, dy_ref[n], preferred_element_type=F32).astype(BF16)
        rows = slice(n * rank, (n + 1) * rank)
        for h in range(2):
            o_ref[h, rows, :] = grad[:, h * half : (h + 1) * half]


def gradients(rot, dy):
    count, tokens, width = dy.shape
    rank = rot.shape[1]
    return pl.pallas_call(
        grad_kernel,
        in_specs=[WHOLE, WHOLE],
        out_specs=WHOLE,
        out_shape=jax.ShapeDtypeStruct((2, count * rank, width // 2), BF16),
        compiler_params=params(),
        cost_estimate=pl.CostEstimate(
            flops=2 * count * tokens * width * rank, bytes_accessed=3 << 20, transcendentals=0
        ),
    )(rot, dy)


def coef_parts(ids_ref, q_ref, pieces, offsets, dests):
    z, x_hi, x_lo = ids_ref[0], ids_ref[1], ids_ref[2]
    blocks = [lax.rem(z + off + 8, 8) for off in offsets]
    for i, (other_hi, other_lo) in enumerate(dests):
        j = 1 - x_lo if other_lo else x_lo
        half = 1 - x_hi if other_hi else x_hi
        cols = pl.ds(pl.multiple_of(half * 256, 256), 256)
        for h in range(2):
            rows = slice(256 * h, 256 * h + 256)
            total = None
            for piece, b in zip(pieces, blocks):
                term = jnp.dot(piece[h], q_ref[b, j, :, cols], preferred_element_type=F32)
                total = term if total is None else total + term
            yield i, rows, total


DESTS = ((1, 0), (0, 1), (1, 1), (0, 0))
COEF = (512, 256)


def early_kernel(offsets, ids_ref, q_ref, *refs):
    pieces, out = refs[:-1], refs[-1]
    for i, rows, total in coef_parts(ids_ref, q_ref, pieces, offsets, DESTS):
        out[i, rows, :] = total


def late_kernel(offset, ids_ref, q_ref, piece_ref, sum_ref, away_ref, keep_ref):
    for i, rows, total in coef_parts(ids_ref, q_ref, [piece_ref], [offset], DESTS):
        total = sum_ref[i, rows, :] + total
        if i == 3:
            keep_ref[rows, :] = total
        hi, lo = DESTS[i]
        slot = (1 - ids_ref[1] if hi else ids_ref[1]) * 2 + (1 - ids_ref[2] if lo else ids_ref[2])
        away_ref[slot, rows, :] = total.astype(BF16)


def early(ids, basis, pieces, offsets):
    return pl.pallas_call(
        functools.partial(early_kernel, offsets),
        in_specs=[SCALARS] + [WHOLE] * (1 + len(pieces)),
        out_specs=WHOLE,
        out_shape=jax.ShapeDtypeStruct((4,) + COEF, F32),
        compiler_params=params(),
        cost_estimate=pl.CostEstimate(flops=2 << 30, bytes_accessed=8 << 20, transcendentals=0),
    )(ids, basis, *pieces)


def late(ids, basis, piece, offset, sums):
    return pl.pallas_call(
        functools.partial(late_kernel, offset),
        in_specs=[SCALARS] + [WHOLE] * 3,
        out_specs=[WHOLE] * 2,
        out_shape=[
            jax.ShapeDtypeStruct((4,) + COEF, BF16),
            jax.ShapeDtypeStruct(COEF, F32),
        ],
        compiler_params=params(),
        cost_estimate=pl.CostEstimate(flops=1 << 28, bytes_accessed=2 << 20, transcendentals=0),
    )(ids, basis, piece, sums)


def square_kernel(ids_ref, keep_ref, p_ref, o_ref):
    x_hi, x_lo = ids_ref[1], ids_ref[2]
    far, beside = 2 * (1 - x_hi) + x_lo, 2 * x_hi + 1 - x_lo
    across = 2 * (1 - x_hi) + 1 - x_lo
    coef = keep_ref[...]
    for slot in (far, beside, across):
        coef = coef + p_ref[slot].astype(F32)
    sq = coef * coef
    rank = o_ref.shape[1]
    total = sq[:rank]
    for n in range(1, sq.shape[0] // rank):
        total = total + sq[n * rank : (n + 1) * rank]
    total = total.astype(BF16)
    for i in range(o_ref.shape[0]):
        o_ref[i] = total


def mean_kernel(p_ref, o_ref):
    total = p_ref[0].astype(F32)
    for i in range(1, p_ref.shape[0]):
        total = total + p_ref[i].astype(F32)
    o_ref[...] = total * (1.0 / 128)


def add_kernel(p_ref, o_ref):
    o_ref[...] = p_ref[0] + p_ref[1]


def join_kernel(p_ref, o_ref):
    half = p_ref.shape[2]
    for h in range(2):
        o_ref[:, h * half : (h + 1) * half] = p_ref[h]


def swap(x, axis, stride=1):
    size = dict(zip(DP + EIGEN, SIZES))[axis]
    return lax.ppermute(x, axis, [(i, i ^ stride) for i in range(size)])


def shift(x, step):
    return lax.ppermute(x, "z", [(i, (i + step) % 8) for i in range(8)])


TURN = [(4 * h + 2 * c + l, 4 * c + 2 * l + h) for h in range(2) for c in range(2) for l in range(2)]


def shards(inputs, out_grads, down, out_basis, adapter_basis):
    z = lax.axis_index("z")
    x_hi, x_lo = lax.axis_index("x_hi"), lax.axis_index("x_lo")
    ids = jnp.stack([z, x_hi, x_lo]).astype(jnp.int32)

    turned = lax.ppermute(out_basis, ("x_hi", "core", "x_lo"), TURN)
    parts = project(inputs, down)
    parts = lax.all_to_all(parts, EIGEN, 0, 0)
    parts = rotate(parts, adapter_basis)
    parts, turned = lax.optimization_barrier((parts, turned))
    basis = lax.all_gather(turned, ("y", "core"), axis=0).reshape(8, 2, *out_basis.shape)
    rot = lax.all_to_all(parts, EIGEN, 0, 0)

    piece = lax.all_to_all(gradients(rot, out_grads), "x_hi", 0, 0)
    pieces, offsets = [piece], [0]
    up = down_ = piece
    for s in range(1, 4):
        up, down_ = shift(up, 1), shift(down_, -1)
        pieces += [up, down_]
        offsets += [-s, s]
    last = shift(up, 1)

    sums = early(ids, basis, pieces, offsets)
    away, keep = late(ids, basis, last, 4, sums)
    away = lax.all_to_all(away, ("x_hi", "x_lo"), 0, 0)
    sums = pl.pallas_call(
        square_kernel,
        in_specs=[SCALARS] + [WHOLE] * 2,
        out_specs=WHOLE,
        out_shape=jax.ShapeDtypeStruct((8, 64, 256), BF16),
        compiler_params=params(),
    )(ids, keep, away)
    sums = lax.all_to_all(sums, "y", 0, 0)
    mean = pl.pallas_call(
        mean_kernel,
        in_specs=[WHOLE],
        out_specs=WHOLE,
        out_shape=jax.ShapeDtypeStruct((64, 256), F32),
        compiler_params=params(),
    )(sums)
    mean = pl.pallas_call(
        add_kernel,
        in_specs=[WHOLE],
        out_specs=WHOLE,
        out_shape=jax.ShapeDtypeStruct((64, 256), F32),
        compiler_params=params(),
    )(lax.all_gather(mean, "core", axis=0))
    mean = lax.all_gather(mean, "x_hi", axis=0)
    return pl.pallas_call(
        join_kernel,
        in_specs=[WHOLE],
        out_specs=WHOLE,
        out_shape=jax.ShapeDtypeStruct((64, 512), F32),
        compiler_params=params(),
    )(mean)


def solution(mesh):
    fine = Mesh(mesh.devices.reshape(SIZES), DP + EIGEN)
    return jax.shard_map(
        shards,
        mesh=fine,
        in_specs=(
            P(DP, None, EIGEN),
            P(DP, None, EIGEN),
            P(None, EIGEN),
            P(DP, EIGEN),
            P(),
        ),
        out_specs=P(None, EIGEN),
        check_vma=False,
    )
```

```python
import functools

import jax
import jax.numpy as jnp
from jax import lax
from jax.experimental import pallas as pl
from jax.experimental.pallas import tpu as pltpu
from jax.sharding import Mesh, PartitionSpec as P

DP = ("x_hi", "y", "core")
EIGEN = ("x_lo", "z")
SIZES = (2, 8, 2, 2, 8)
F32, BF16 = jnp.float32, jnp.bfloat16
PARTIAL = BF16
VMEM_LIMIT = 16 * 1024 * 1024


def params(**kw):
    return pltpu.CompilerParams(vmem_limit_bytes=VMEM_LIMIT, **kw)


WHOLE = pl.BlockSpec(memory_space=pltpu.VMEM)
SCALARS = pl.BlockSpec(memory_space=pltpu.SMEM)


HBM = pl.BlockSpec(memory_space=pltpu.HBM)


def project_kernel(a_ref, x_ref, o_ref, a_buf, x_buf, sems):
    count = x_ref.shape[0]
    per = o_ref.shape[0] // count
    down = pltpu.make_async_copy(a_ref, a_buf, sems.at[count])
    down.start()
    copies = [pltpu.make_async_copy(x_ref.at[n], x_buf.at[n], sems.at[n]) for n in range(count)]
    for copy in copies:
        copy.start()
    down.wait()
    for n in range(count):
        copies[n].wait()
        got = lax.dot_general(
            a_buf[...], x_buf[n], (((1,), (1,)), ((), ())), preferred_element_type=F32
        )
        for c in range(per):
            o_ref[n * per + c] = got[:, c * 128 : (c + 1) * 128].astype(o_ref.dtype)


def project(inputs, down):
    count, tokens, width = inputs.shape
    rank = down.shape[0]
    return pl.pallas_call(
        project_kernel,
        in_specs=[HBM, HBM],
        out_specs=WHOLE,
        out_shape=jax.ShapeDtypeStruct((count * tokens // 128, rank, 128), PARTIAL),
        scratch_shapes=[
            pltpu.VMEM(down.shape, BF16),
            pltpu.VMEM(inputs.shape, BF16),
            pltpu.SemaphoreType.DMA((count + 1,)),
        ],
        compiler_params=pltpu.CompilerParams(vmem_limit_bytes=60 * 1024 * 1024),
        cost_estimate=pl.CostEstimate(
            flops=2 * count * tokens * width * rank, bytes_accessed=3 << 20, transcendentals=0
        ),
    )(down, inputs)


def rotate_kernel(p_ref, e_ref, o_ref):
    total = p_ref[0].astype(F32)
    for c in range(1, p_ref.shape[0]):
        total = total + p_ref[c].astype(F32)
    rot = lax.dot_general(
        e_ref[...], total.astype(BF16), (((0,), (0,)), ((), ())), preferred_element_type=F32
    ).astype(BF16)
    for c in range(o_ref.shape[0]):
        o_ref[c] = rot


def rotate(parts, basis):
    return pl.pallas_call(
        rotate_kernel,
        in_specs=[WHOLE, WHOLE],
        out_specs=WHOLE,
        out_shape=jax.ShapeDtypeStruct(parts.shape, BF16),
        compiler_params=params(),
    )(parts, basis)


def grad_kernel(rot_ref, dy_ref, o_ref):
    count, rank = dy_ref.shape[0], rot_ref.shape[1]
    per = rot_ref.shape[0] // count
    half = dy_ref.shape[2] // 2
    for n in range(count):
        rot = jnp.concatenate([rot_ref[n * per + c] for c in range(per)], axis=1)
        grad = jnp.dot(rot, dy_ref[n], preferred_element_type=F32).astype(BF16)
        rows = slice(n * rank, (n + 1) * rank)
        for h in range(2):
            o_ref[h, rows, :] = grad[:, h * half : (h + 1) * half]


def gradients(rot, dy):
    count, tokens, width = dy.shape
    rank = rot.shape[1]
    return pl.pallas_call(
        grad_kernel,
        in_specs=[WHOLE, WHOLE],
        out_specs=WHOLE,
        out_shape=jax.ShapeDtypeStruct((2, count * rank, width // 2), BF16),
        compiler_params=params(),
        cost_estimate=pl.CostEstimate(
            flops=2 * count * tokens * width * rank, bytes_accessed=3 << 20, transcendentals=0
        ),
    )(rot, dy)


def coef_parts(ids_ref, q_ref, pieces, offsets, dests):
    z, x_hi, x_lo = ids_ref[0], ids_ref[1], ids_ref[2]
    blocks = [lax.rem(z + off + 8, 8) for off in offsets]
    for i, (other_hi, other_lo) in enumerate(dests):
        j = 1 - x_lo if other_lo else x_lo
        half = 1 - x_hi if other_hi else x_hi
        cols = pl.ds(pl.multiple_of(half * 256, 256), 256)
        for h in range(2):
            rows = slice(256 * h, 256 * h + 256)
            total = None
            for piece, b in zip(pieces, blocks):
                term = jnp.dot(piece[h], q_ref[b, j, :, cols], preferred_element_type=F32)
                total = term if total is None else total + term
            yield i, rows, total


DESTS = ((1, 0), (0, 1), (1, 1), (0, 0))
COEF = (512, 256)


def early_kernel(offsets, ids_ref, q_ref, *refs):
    pieces, out = refs[:-1], refs[-1]
    for i, rows, total in coef_parts(ids_ref, q_ref, pieces, offsets, DESTS):
        out[i, rows, :] = total


def late_kernel(offset, ids_ref, q_ref, piece_ref, sum_ref, away_ref, keep_ref):
    for i, rows, total in coef_parts(ids_ref, q_ref, [piece_ref], [offset], DESTS):
        total = sum_ref[i, rows, :] + total
        if i == 3:
            keep_ref[rows, :] = total
        hi, lo = DESTS[i]
        slot = (1 - ids_ref[2] if lo else ids_ref[2]) * 2 + (1 - ids_ref[1] if hi else ids_ref[1])
        away_ref[slot, rows, :] = total.astype(BF16)


def early(ids, basis, pieces, offsets):
    return pl.pallas_call(
        functools.partial(early_kernel, offsets),
        in_specs=[SCALARS] + [WHOLE] * (1 + len(pieces)),
        out_specs=WHOLE,
        out_shape=jax.ShapeDtypeStruct((4,) + COEF, F32),
        compiler_params=params(),
        cost_estimate=pl.CostEstimate(flops=2 << 30, bytes_accessed=8 << 20, transcendentals=0),
    )(ids, basis, *pieces)


def late(ids, basis, piece, offset, sums):
    return pl.pallas_call(
        functools.partial(late_kernel, offset),
        in_specs=[SCALARS] + [WHOLE] * 3,
        out_specs=[WHOLE] * 2,
        out_shape=[
            jax.ShapeDtypeStruct((4,) + COEF, BF16),
            jax.ShapeDtypeStruct(COEF, F32),
        ],
        compiler_params=params(),
        cost_estimate=pl.CostEstimate(flops=1 << 28, bytes_accessed=2 << 20, transcendentals=0),
    )(ids, basis, piece, sums)


def square_kernel(ids_ref, keep_ref, p_ref, o_ref):
    x_hi, x_lo = ids_ref[1], ids_ref[2]
    far, beside = 2 * x_lo + 1 - x_hi, 2 * (1 - x_lo) + x_hi
    across = 2 * (1 - x_lo) + 1 - x_hi
    coef = keep_ref[...]
    for slot in (far, beside, across):
        coef = coef + p_ref[slot].astype(F32)
    sq = coef * coef
    rank = o_ref.shape[1]
    total = sq[:rank]
    for n in range(1, sq.shape[0] // rank):
        total = total + sq[n * rank : (n + 1) * rank]
    total = total.astype(BF16)
    for i in range(o_ref.shape[0]):
        o_ref[i] = total


def mean_kernel(p_ref, o_ref):
    total = p_ref[0].astype(F32)
    for i in range(1, p_ref.shape[0]):
        total = total + p_ref[i].astype(F32)
    o_ref[...] = total * (1.0 / 128)


def add_kernel(p_ref, o_ref):
    o_ref[...] = p_ref[0] + p_ref[1]


def join_kernel(p_ref, o_ref):
    half = p_ref.shape[2]
    for h in range(2):
        o_ref[:, h * half : (h + 1) * half] = p_ref[h]


def swap(x, axis, stride=1):
    size = dict(zip(DP + EIGEN, SIZES))[axis]
    return lax.ppermute(x, axis, [(i, i ^ stride) for i in range(size)])


def shift(x, step):
    return lax.ppermute(x, "z", [(i, (i + step) % 8) for i in range(8)])


TURN = [(4 * h + 2 * c + l, 4 * c + 2 * l + h) for h in range(2) for c in range(2) for l in range(2)]


def shards(inputs, out_grads, down, out_basis, adapter_basis):
    z = lax.axis_index("z")
    x_hi, x_lo = lax.axis_index("x_hi"), lax.axis_index("x_lo")
    ids = jnp.stack([z, x_hi, x_lo]).astype(jnp.int32)

    turned = lax.ppermute(out_basis, ("x_hi", "core", "x_lo"), TURN)
    parts = project(inputs, down)
    parts = lax.all_to_all(parts, EIGEN, 0, 0)
    parts = rotate(parts, adapter_basis)
    parts, turned = lax.optimization_barrier((parts, turned))
    basis = lax.all_gather(turned, ("y", "core"), axis=0).reshape(8, 2, *out_basis.shape)
    rot = lax.all_to_all(parts, EIGEN, 0, 0)

    piece = lax.all_to_all(gradients(rot, out_grads), "x_hi", 0, 0)
    pieces, offsets = [piece], [0]
    up = down_ = piece
    for s in range(1, 4):
        up, down_ = shift(up, 1), shift(down_, -1)
        pieces += [up, down_]
        offsets += [-s, s]
    last = shift(up, 1)

    sums = early(ids, basis, pieces, offsets)
    away, keep = late(ids, basis, last, 4, sums)
    away = lax.all_to_all(away, ("x_lo", "x_hi"), 0, 0)
    sums = pl.pallas_call(
        square_kernel,
        in_specs=[SCALARS] + [WHOLE] * 2,
        out_specs=WHOLE,
        out_shape=jax.ShapeDtypeStruct((8, 64, 256), BF16),
        compiler_params=params(),
    )(ids, keep, away)
    sums = lax.all_to_all(sums, "y", 0, 0)
    mean = pl.pallas_call(
        mean_kernel,
        in_specs=[WHOLE],
        out_specs=WHOLE,
        out_shape=jax.ShapeDtypeStruct((64, 256), F32),
        compiler_params=params(),
    )(sums)
    mean = pl.pallas_call(
        add_kernel,
        in_specs=[WHOLE],
        out_specs=WHOLE,
        out_shape=jax.ShapeDtypeStruct((64, 256), F32),
        compiler_params=params(),
    )(lax.all_gather(mean, "core", axis=0))
    mean = lax.all_gather(mean, "x_hi", axis=0)
    return pl.pallas_call(
        join_kernel,
        in_specs=[WHOLE],
        out_specs=WHOLE,
        out_shape=jax.ShapeDtypeStruct((64, 512), F32),
        compiler_params=params(),
    )(mean)


def solution(mesh):
    fine = Mesh(mesh.devices.reshape(SIZES), DP + EIGEN)
    return jax.shard_map(
        shards,
        mesh=fine,
        in_specs=(
            P(DP, None, EIGEN),
            P(DP, None, EIGEN),
            P(None, EIGEN),
            P(DP, EIGEN),
            P(),
        ),
        out_specs=P(None, EIGEN),
        check_vma=False,
    )
```

```python
import functools

import jax
import jax.numpy as jnp
from jax import lax
from jax.experimental import pallas as pl
from jax.experimental.pallas import tpu as pltpu
from jax.sharding import Mesh, PartitionSpec as P

DP = ("x_hi", "y", "core")
EIGEN = ("x_lo", "z")
SIZES = (2, 8, 2, 2, 8)
F32, BF16 = jnp.float32, jnp.bfloat16
PARTIAL = BF16
VMEM_LIMIT = 16 * 1024 * 1024


def params(**kw):
    return pltpu.CompilerParams(vmem_limit_bytes=VMEM_LIMIT, **kw)


WHOLE = pl.BlockSpec(memory_space=pltpu.VMEM)
SCALARS = pl.BlockSpec(memory_space=pltpu.SMEM)


HBM = pl.BlockSpec(memory_space=pltpu.HBM)


def project_kernel(a_ref, x_ref, o_ref, a_buf, x_buf, sems):
    count = x_ref.shape[0]
    per = o_ref.shape[0] // count
    down = pltpu.make_async_copy(a_ref, a_buf, sems.at[count])
    down.start()
    copies = [pltpu.make_async_copy(x_ref.at[n], x_buf.at[n], sems.at[n]) for n in range(count)]
    for copy in copies:
        copy.start()
    down.wait()
    for n in range(count):
        copies[n].wait()
        got = lax.dot_general(
            a_buf[...], x_buf[n], (((1,), (1,)), ((), ())), preferred_element_type=F32
        )
        for c in range(per):
            o_ref[n * per + c] = got[:, c * 128 : (c + 1) * 128].astype(o_ref.dtype)


def project(inputs, down):
    count, tokens, width = inputs.shape
    rank = down.shape[0]
    return pl.pallas_call(
        project_kernel,
        in_specs=[HBM, HBM],
        out_specs=WHOLE,
        out_shape=jax.ShapeDtypeStruct((count * tokens // 128, rank, 128), PARTIAL),
        scratch_shapes=[
            pltpu.VMEM(down.shape, BF16),
            pltpu.VMEM(inputs.shape, BF16),
            pltpu.SemaphoreType.DMA((count + 1,)),
        ],
        compiler_params=pltpu.CompilerParams(vmem_limit_bytes=60 * 1024 * 1024),
        cost_estimate=pl.CostEstimate(
            flops=2 * count * tokens * width * rank, bytes_accessed=3 << 20, transcendentals=0
        ),
    )(down, inputs)


def rotate_kernel(p_ref, e_ref, o_ref):
    total = p_ref[0].astype(F32)
    for c in range(1, p_ref.shape[0]):
        total = total + p_ref[c].astype(F32)
    rot = lax.dot_general(
        e_ref[...], total.astype(BF16), (((0,), (0,)), ((), ())), preferred_element_type=F32
    ).astype(BF16)
    for c in range(o_ref.shape[0]):
        o_ref[c] = rot


def rotate(parts, basis):
    return pl.pallas_call(
        rotate_kernel,
        in_specs=[WHOLE, WHOLE],
        out_specs=WHOLE,
        out_shape=jax.ShapeDtypeStruct(parts.shape, BF16),
        compiler_params=params(),
    )(parts, basis)


def grad_kernel(rot_ref, dy_ref, o_ref):
    count, rank = dy_ref.shape[0], rot_ref.shape[1]
    per = rot_ref.shape[0] // count
    half = dy_ref.shape[2] // 2
    for n in range(count):
        rot = jnp.concatenate([rot_ref[n * per + c] for c in range(per)], axis=1)
        grad = jnp.dot(rot, dy_ref[n], preferred_element_type=F32).astype(BF16)
        rows = slice(n * rank, (n + 1) * rank)
        for h in range(2):
            o_ref[h, rows, :] = grad[:, h * half : (h + 1) * half]


def gradients(rot, dy):
    count, tokens, width = dy.shape
    rank = rot.shape[1]
    return pl.pallas_call(
        grad_kernel,
        in_specs=[WHOLE, WHOLE],
        out_specs=WHOLE,
        out_shape=jax.ShapeDtypeStruct((2, count * rank, width // 2), BF16),
        compiler_params=params(),
        cost_estimate=pl.CostEstimate(
            flops=2 * count * tokens * width * rank, bytes_accessed=3 << 20, transcendentals=0
        ),
    )(rot, dy)


def coef_parts(ids_ref, q_ref, pieces, offsets, dests):
    z, x_hi, x_lo = ids_ref[0], ids_ref[1], ids_ref[2]
    blocks = [lax.rem(z + off + 8, 8) for off in offsets]
    for i, (other_hi, other_lo) in enumerate(dests):
        j = 1 - x_lo if other_lo else x_lo
        half = 1 - x_hi if other_hi else x_hi
        cols = pl.ds(pl.multiple_of(half * 256, 256), 256)
        for h in range(2):
            rows = slice(256 * h, 256 * h + 256)
            total = None
            for piece, b in zip(pieces, blocks):
                term = jnp.dot(piece[h], q_ref[b, j, :, cols], preferred_element_type=F32)
                total = term if total is None else total + term
            yield i, rows, total


DESTS = ((1, 0), (0, 1), (1, 1), (0, 0))
COEF = (512, 256)


def early_kernel(offsets, ids_ref, q_ref, *refs):
    pieces, out = refs[:-1], refs[-1]
    for i, rows, total in coef_parts(ids_ref, q_ref, pieces, offsets, DESTS):
        out[i, rows, :] = total


def late_kernel(offset, ids_ref, q_ref, piece_ref, sum_ref, away_ref, keep_ref):
    for i, rows, total in coef_parts(ids_ref, q_ref, [piece_ref], [offset], DESTS):
        total = sum_ref[i, rows, :] + total
        if i == 3:
            keep_ref[rows, :] = total
        hi, lo = DESTS[i]
        slot = (1 - ids_ref[1] if hi else ids_ref[1]) * 2 + (1 - ids_ref[2] if lo else ids_ref[2])
        away_ref[slot, rows, :] = total.astype(BF16)


def early(ids, basis, pieces, offsets):
    return pl.pallas_call(
        functools.partial(early_kernel, offsets),
        in_specs=[SCALARS] + [WHOLE] * (1 + len(pieces)),
        out_specs=WHOLE,
        out_shape=jax.ShapeDtypeStruct((4,) + COEF, F32),
        compiler_params=params(),
        cost_estimate=pl.CostEstimate(flops=2 << 30, bytes_accessed=8 << 20, transcendentals=0),
    )(ids, basis, *pieces)


def late(ids, basis, piece, offset, sums):
    return pl.pallas_call(
        functools.partial(late_kernel, offset),
        in_specs=[SCALARS] + [WHOLE] * 3,
        out_specs=[WHOLE] * 2,
        out_shape=[
            jax.ShapeDtypeStruct((4,) + COEF, BF16),
            jax.ShapeDtypeStruct(COEF, F32),
        ],
        compiler_params=params(),
        cost_estimate=pl.CostEstimate(flops=1 << 28, bytes_accessed=2 << 20, transcendentals=0),
    )(ids, basis, piece, sums)


def square_kernel(ids_ref, keep_ref, p_ref, o_ref):
    x_hi, x_lo = ids_ref[1], ids_ref[2]
    far, beside = 2 * (1 - x_hi) + x_lo, 2 * x_hi + 1 - x_lo
    across = 2 * (1 - x_hi) + 1 - x_lo
    coef = keep_ref[...]
    for slot in (far, beside, across):
        coef = coef + p_ref[slot].astype(F32)
    sq = coef * coef
    rank = o_ref.shape[1]
    total = sq[:rank]
    for n in range(1, sq.shape[0] // rank):
        total = total + sq[n * rank : (n + 1) * rank]
    total = total.astype(BF16)
    for i in range(o_ref.shape[0]):
        o_ref[i] = total


def mean_kernel(p_ref, o_ref):
    total = p_ref[0].astype(F32)
    for i in range(1, p_ref.shape[0]):
        total = total + p_ref[i].astype(F32)
    o_ref[...] = total * (1.0 / 128)


def add_kernel(p_ref, o_ref):
    o_ref[...] = p_ref[0] + p_ref[1]


def join_kernel(p_ref, o_ref):
    half = p_ref.shape[2]
    for h in range(2):
        o_ref[:, h * half : (h + 1) * half] = p_ref[h]


def swap(x, axis, stride=1):
    size = dict(zip(DP + EIGEN, SIZES))[axis]
    return lax.ppermute(x, axis, [(i, i ^ stride) for i in range(size)])


def shift(x, step):
    return lax.ppermute(x, "z", [(i, (i + step) % 8) for i in range(8)])


TURN = [(4 * h + 2 * c + l, 4 * c + 2 * l + h) for h in range(2) for c in range(2) for l in range(2)]


def shards(inputs, out_grads, down, out_basis, adapter_basis):
    z = lax.axis_index("z")
    x_hi, x_lo = lax.axis_index("x_hi"), lax.axis_index("x_lo")
    ids = jnp.stack([z, x_hi, x_lo]).astype(jnp.int32)

    turned = lax.ppermute(out_basis, ("x_hi", "core", "x_lo"), TURN)
    parts = project(inputs, down)
    parts = lax.all_to_all(parts, EIGEN, 0, 0)
    parts, turned = lax.optimization_barrier((parts, turned))
    basis = lax.all_gather(turned, ("y", "core"), axis=0).reshape(8, 2, *out_basis.shape)
    rot = lax.all_to_all(rotate(parts, adapter_basis), EIGEN, 0, 0)

    piece = lax.all_to_all(gradients(rot, out_grads), "x_hi", 0, 0)
    pieces, offsets = [piece], [0]
    up = down_ = piece
    for s in range(1, 4):
        up, down_ = shift(up, 1), shift(down_, -1)
        pieces += [up, down_]
        offsets += [-s, s]
    last = shift(up, 1)

    sums = early(ids, basis, pieces, offsets)
    away, keep = late(ids, basis, last, 4, sums)
    away = lax.all_to_all(away, ("x_hi", "x_lo"), 0, 0)
    sums = pl.pallas_call(
        square_kernel,
        in_specs=[SCALARS] + [WHOLE] * 2,
        out_specs=WHOLE,
        out_shape=jax.ShapeDtypeStruct((8, 64, 256), BF16),
        compiler_params=params(),
    )(ids, keep, away)
    sums = lax.all_to_all(sums, "y", 0, 0)
    mean = pl.pallas_call(
        mean_kernel,
        in_specs=[WHOLE],
        out_specs=WHOLE,
        out_shape=jax.ShapeDtypeStruct((64, 256), F32),
        compiler_params=params(),
    )(sums)
    mean = pl.pallas_call(
        add_kernel,
        in_specs=[WHOLE],
        out_specs=WHOLE,
        out_shape=jax.ShapeDtypeStruct((64, 256), F32),
        compiler_params=params(),
    )(lax.all_gather(mean, "core", axis=0))
    mean = lax.all_gather(mean, "x_hi", axis=0)
    return pl.pallas_call(
        join_kernel,
        in_specs=[WHOLE],
        out_specs=WHOLE,
        out_shape=jax.ShapeDtypeStruct((64, 512), F32),
        compiler_params=params(),
    )(mean)


def solution(mesh):
    fine = Mesh(mesh.devices.reshape(SIZES), DP + EIGEN)
    return jax.shard_map(
        shards,
        mesh=fine,
        in_specs=(
            P(DP, None, EIGEN),
            P(DP, None, EIGEN),
            P(None, EIGEN),
            P(DP, EIGEN),
            P(),
        ),
        out_specs=P(None, EIGEN),
        check_vma=False,
    )
```
